256 devices in a mesh: dp: 8 (over y_lo, x), expert: 32 (over y_hi, z, core).
Axes of the slice: x: 4, y: 4 (y_hi: 2, y_lo: 2; y = y_hi * 2 + y_lo), z: 8, core: 2. Of those that a mesh axis runs over, the one named last changes fastest.
Arguments:
- tokens: bfloat16 [512, 256, 1280], P(('dp', 'expert')), may hold values from -40 to 40
- router: bfloat16 [32, 1280], replicated, may hold values from -1 to 1
- w_in: bfloat16 [32, 1280, 5120], P('expert', None, 'dp'), may hold values from -0.15625 to 0.15625
- w_out: bfloat16 [32, 5120, 1280], P('expert', 'dp'), may hold values from -0.078125 to 0.078125
- cotangent: bfloat16 [512, 256, 1280], P(('dp', 'expert')), may hold values from -6 to 6
Outputs:
- output: bfloat16 [512, 256, 1280], P(('dp', 'expert'))
- grad_tokens: bfloat16 [512, 256, 1280], P(('dp', 'expert'))
- grad_router: float32 [32, 1280], replicated
- grad_in: bfloat16 [32, 1280, 5120], P('expert', None, 'dp')
- grad_out: bfloat16 [32, 5120, 1280], P('expert', 'dp')
The draws below stay inside these ranges and needn't reach their ends.
All inputs are finite; a program needn't handle non-finite values.
Results may differ from the reference program's by a relative error of at most 0.03.
Values may be sent and summed in bfloat16 or wider, within the bound.
No kernel may reach another device: no remote copies, remote signals or barrier semaphores. Data moves between devices by JAX's collectives and lax.ppermute only.
A program may use at most 64 MiB of HBM per device.

```python
import math
import jax
import jax.numpy as jnp
from jax import lax

D = 1280
FF = 5120
M = 256
EXPERTS = 32
FF_DEV = 640
IMAGES = 512
N_DP = 8


def walsh_router(key):
    width_bits = min((D & -D).bit_length() - 1, 8)
    sign_flips = jnp.where(jax.random.bernoulli(jax.random.fold_in(key, 11), 0.5, (D,)), 1.0, -1.0).astype(jnp.float32)
    walsh_codes = jax.random.permutation(jax.random.fold_in(key, 12), 2 ** width_bits)[:EXPERTS].astype(jnp.int32)
    column_index = jnp.arange(D, dtype=jnp.int32)
    shared_bits = jnp.bitwise_and(column_index[None, :], walsh_codes[:, None])
    parity = jnp.zeros(shared_bits.shape, jnp.int32)
    for bit_shift in range(width_bits):
        parity = parity + jnp.bitwise_and(jnp.right_shift(shared_bits, bit_shift), 1)
    pattern = (1 - 2 * (parity % 2)).astype(jnp.float32)
    return pattern * sign_flips[None, :] * (2.5 / math.sqrt(D))


def draw_router(key, part):
    return walsh_router(key).astype(jnp.bfloat16)


def draw_tokens(key, part):
    key = jax.random.fold_in(key, 3)
    values = jax.random.normal(jax.random.fold_in(key, 1), (IMAGES, M, D), jnp.float32)
    return jnp.clip(values, -40.0, 40.0).astype(jnp.bfloat16)


def shard_levels(own_key, dims, split, low, top_value):
    def one(dim, shards_of):
        heights = jax.random.uniform(jax.random.fold_in(jax.random.fold_in(own_key, 6), dim), (shards_of,), jnp.float32, low / len(split), top_value / len(split))
        return jnp.repeat(jnp.exp(heights), dims[dim] // shards_of).reshape((-1,) + (1,) * (len(dims) - dim - 1))

    level = one(*split[0])
    for cut in split[1:]:
        level = level * one(*cut)
    return level


def bell_draw(key, extent, spread, reach, split=(), kind=jnp.bfloat16):
    drawn = spread * jax.random.normal(key, extent, jnp.float32)
    if split:
        drawn = drawn * shard_levels(key, extent, split, -0.22, 0.18)
    return jnp.clip(drawn, -reach, reach).astype(kind)


def setup_inputs(seed: int = 0) -> dict:
    key_list = jax.random.split(jax.random.key(seed), 6)
    return {
        "tokens": draw_tokens(jax.random.fold_in(key_list[5], 71), 0),
        "router": draw_router(jax.random.fold_in(key_list[5], 71), 0),
        "w_in": bell_draw(key_list[2], (EXPERTS, D, FF), D ** -0.5, 0.15625, ((0, 32), (2, 8))),
        "w_out": bell_draw(key_list[3], (EXPERTS, FF, D), FF ** -0.5, 0.078125, ((0, 32), (1, 8))),
        "cotangent": bell_draw(key_list[4], (IMAGES, M, D), 1.0, 6.0, ((0, 256),)),
    }


def reference(tokens, router, w_in, w_out, cotangent):
    f32 = jnp.float32
    bf16 = jnp.bfloat16
    tok_f = tokens.astype(f32)
    router_f = router.astype(f32)
    logits = jnp.einsum('bmd,sd->bsm', tok_f, router_f)
    disp_prob = jax.nn.softmax(logits, axis=2)
    comb_prob = jax.nn.softmax(logits, axis=1)
    dispatch = disp_prob.astype(bf16)
    combine = comb_prob.astype(bf16)
    slots_in = jnp.einsum('bsm,bmd->bsd', dispatch.astype(f32), tok_f).astype(bf16)
    preact = jnp.einsum('bsd,sdf->bsf', slots_in.astype(f32), w_in.astype(f32))
    hidden = jax.nn.gelu(preact).astype(bf16)
    total_out = jnp.zeros(slots_in.shape, f32)
    for block_index in range(N_DP):
        first_unit = block_index * FF_DEV
        term = jnp.einsum('bsf,sfd->bsd', hidden[:, :, first_unit:first_unit + FF_DEV].astype(f32), w_out[:, first_unit:first_unit + FF_DEV, :].astype(f32))
        total_out = total_out + lax.optimization_barrier(term.astype(bf16)).astype(f32)
    slots_out = total_out.astype(bf16)
    output = jnp.einsum('bsm,bsd->bmd', combine.astype(f32), slots_out.astype(f32)).astype(bf16)
    grad_f = cotangent.astype(f32)
    grad_comb = jnp.einsum('bmd,bsd->bsm', grad_f, slots_out.astype(f32))
    grad_slots_out = jnp.einsum('bsm,bmd->bsd', combine.astype(f32), grad_f).astype(bf16)
    grad_hidden = jnp.einsum('bsd,sfd->bsf', grad_slots_out.astype(f32), w_out.astype(f32))
    grad_out = jnp.einsum('bsf,bsd->sfd', hidden.astype(f32), grad_slots_out.astype(f32)).astype(bf16)
    _, pullback = jax.vjp(jax.nn.gelu, preact)
    grad_preact = pullback(grad_hidden)[0].astype(bf16)
    grad_in = jnp.einsum('bsd,bsf->sdf', slots_in.astype(f32), grad_preact.astype(f32)).astype(bf16)
    total_in = jnp.zeros(slots_in.shape, f32)
    for block_index in range(N_DP):
        first_unit = block_index * FF_DEV
        term = jnp.einsum('bsf,sdf->bsd', grad_preact[:, :, first_unit:first_unit + FF_DEV].astype(f32), w_in[:, :, first_unit:first_unit + FF_DEV].astype(f32))
        total_in = total_in + lax.optimization_barrier(term.astype(bf16)).astype(f32)
    grad_slots_in = total_in.astype(bf16)
    grad_disp = jnp.einsum('bmd,bsd->bsm', tok_f, grad_slots_in.astype(f32))
    grad_logits = comb_prob * (grad_comb - lax.optimization_barrier(jnp.sum(comb_prob * grad_comb, axis=1, keepdims=True)))
    grad_logits = grad_logits + disp_prob * (grad_disp - lax.optimization_barrier(jnp.sum(disp_prob * grad_disp, axis=2, keepdims=True)))
    grad_logits = grad_logits.astype(bf16)
    grad_tokens = jnp.einsum('bsm,bsd->bmd', dispatch.astype(f32), grad_slots_in.astype(f32))
    grad_tokens = grad_tokens + jnp.einsum('bsm,sd->bmd', grad_logits.astype(f32), router_f)
    grad_tokens = grad_tokens.astype(bf16)
    grad_router = jnp.einsum('bsm,bmd->sd', grad_logits.astype(f32), tok_f)
    return (output, grad_tokens, grad_router, grad_in, grad_out)
```

```python
import jax
import jax.numpy as jnp
from jax import lax
from jax.sharding import PartitionSpec as P

BF16 = jnp.bfloat16
F32 = jnp.float32
D = 1280


def dot(spec, a, b):
    return jnp.einsum(spec, a, b, preferred_element_type=F32)


def exchange(x, axis):
    return lax.all_to_all(x, axis, split_axis=0, concat_axis=0, tiled=True)


def copies_to_all(x, axis, n):
    return exchange(jnp.broadcast_to(x[None], (n,) + x.shape), axis)


def sum_over_all(term):
    part = jnp.sum(exchange(term, "expert"), axis=0)
    part = jnp.sum(copies_to_all(part, "dp", 8), axis=0)
    return copies_to_all(part, "expert", 32)


def experts(rows, grad_rows, w_in, w_out):
    preact = dot("bd,df->bf", rows, w_in)
    hidden = jax.nn.gelu(preact).astype(BF16)
    partial_out = dot("bf,fd->bd", hidden, w_out).astype(BF16)
    grad_hidden = dot("bd,fd->bf", grad_rows, w_out)
    _, pullback = jax.vjp(jax.nn.gelu, preact)
    grad_preact = pullback(grad_hidden)[0].astype(BF16)
    partial_in = dot("bf,df->bd", grad_preact, w_in).astype(BF16)
    grad_out = dot("bf,bd->fd", hidden, grad_rows).astype(BF16)
    grad_in = dot("bd,bf->df", rows, grad_preact).astype(BF16)
    return (partial_out, partial_in, grad_in, grad_out)


def shards(tokens, router, w_in, w_out, cotangent):
    logits = dot("bmd,sd->bsm", tokens, router)
    disp_prob = jax.nn.softmax(logits, axis=2)
    comb_prob = jax.nn.softmax(logits, axis=1)
    dispatch = disp_prob.astype(BF16)
    combine = comb_prob.astype(BF16)
    slots_in = dot("bsm,bmd->sbd", dispatch, tokens).astype(BF16)
    grad_slots_out = dot("bsm,bmd->sbd", combine, cotangent).astype(BF16)
    sent = exchange(jnp.concatenate([slots_in, grad_slots_out], axis=2), "expert")
    rows = copies_to_all(sent.reshape(64, 2 * D), "dp", 8).reshape(512, 2 * D)
    partial_out, partial_in, grad_in, grad_out = experts(
        rows[:, :D], rows[:, D:], w_in[0], w_out[0]
    )
    partial = jnp.concatenate([partial_out, partial_in], axis=1).reshape(8, 64, 2 * D)
    summed = jnp.sum(exchange(partial, "dp").astype(F32), axis=0).astype(BF16)
    back = exchange(summed.reshape(32, 2, 2 * D), "expert")
    slots_out = back[:, :, :D]
    grad_slots_in = back[:, :, D:]
    grad_comb = dot("bmd,sbd->bsm", cotangent, slots_out)
    grad_disp = dot("bmd,sbd->bsm", tokens, grad_slots_in)
    grad_logits = comb_prob * (grad_comb - jnp.sum(comb_prob * grad_comb, axis=1, keepdims=True))
    grad_logits = grad_logits + disp_prob * (
        grad_disp - jnp.sum(disp_prob * grad_disp, axis=2, keepdims=True)
    )
    grad_logits = grad_logits.astype(BF16)
    router_term = dot("bsm,bmd->sd", grad_logits, tokens)
    grad_router = sum_over_all(router_term)
    output = dot("bsm,sbd->bmd", combine, slots_out).astype(BF16)
    grad_tokens = dot("bsm,sbd->bmd", dispatch, grad_slots_in)
    grad_tokens = grad_tokens + dot("bsm,sd->bmd", grad_logits, router)
    return (output, grad_tokens.astype(BF16), grad_router, grad_in[None], grad_out[None])


def solution(mesh):
    placed = (
        P(("dp", "expert"), None, None),
        P(),
        P("expert", None, "dp"),
        P("expert", "dp", None),
        P(("dp", "expert"), None, None),
    )
    return jax.shard_map(
        shards,
        mesh=mesh,
        in_specs=placed,
        out_specs=(placed[0], placed[0], P(), placed[2], placed[3]),
        check_vma=False,
    )
```

```python
import functools

import jax
import jax.numpy as jnp
from jax import lax
from jax.experimental import pallas as pl
from jax.experimental.pallas import tpu as pltpu
from jax.sharding import Mesh, PartitionSpec as P

BF16 = jnp.bfloat16
F32 = jnp.float32
D = 1280
M = 256
SLOTS = 32
HID = 640
AXES = ("yl", "x", "yh", "z", "c")
DP = ("yl", "x")
EXPERT = ("yh", "z", "c")
PLANE = ("yl", "x", "c")
COLUMN = ("yh", "z")
VMEM = pl.BlockSpec(memory_space=pltpu.VMEM)
SMEM = pl.BlockSpec(memory_space=pltpu.SMEM)
PARAMS = pltpu.CompilerParams(vmem_limit_bytes=16 * 2**20)


def cost(flops, size):
    return pl.CostEstimate(flops=flops, bytes_accessed=size, transcendentals=0)


def mm(a, b):
    return jnp.dot(a, b, preferred_element_type=F32)


def mm_nt(a, b):
    return lax.dot_general(a, b, (((1,), (1,)), ((), ())), preferred_element_type=F32)


def mm_tn(a, b):
    return lax.dot_general(a, b, (((0,), (0,)), ((), ())), preferred_element_type=F32)


def add(*terms):
    total = terms[0].astype(F32)
    for term in terms[1:]:
        total = total + term.astype(F32)
    return total.astype(BF16)


def exchange(x, axes):
    return lax.all_to_all(x, axes, split_axis=0, concat_axis=0, tiled=True)


def x_up(a):
    return lax.ppermute(a, "x", [(i, (i + 1) % 4) for i in range(4)])


def x_down(a):
    return lax.ppermute(a, "x", [(i, (i + 3) % 4) for i in range(4)])


def y_swap(a):
    return lax.ppermute(a, "yl", [(0, 1), (1, 0)])


def core_swap(a):
    return lax.ppermute(a, "c", [(0, 1), (1, 0)])


def natural_row(r, core):
    slot = 2 * (r >> 3) + (((r >> 2) & 1) ^ core)
    return ((r >> 1) & 1) * 64 + (r & 1) * 32 + slot


def to_message(core, rows):
    r = lax.broadcasted_iota(jnp.int32, (128, 128), 0)
    n = lax.broadcasted_iota(jnp.int32, (128, 128), 1)
    pick = (n == natural_row(r, core)).astype(F32).astype(BF16)
    return mm(pick, rows).astype(BF16)


def from_message(core, message):
    n = lax.broadcasted_iota(jnp.int32, (128, 128), 0)
    r = lax.broadcasted_iota(jnp.int32, (128, 128), 1)
    pick = (n == natural_row(r, core)).astype(F32).astype(BF16)
    return mm(pick, message).astype(BF16)


def route_kernel(core, tokens, router, cotangent, message, probs, rows):
    image = pl.program_id(0)
    tok = tokens[0]
    logits = mm_nt(router[...], tok)
    disp = jnp.exp(logits - jnp.max(logits, axis=1, keepdims=True))
    disp = disp / jnp.sum(disp, axis=1, keepdims=True)
    comb = jnp.exp(logits - jnp.max(logits, axis=0, keepdims=True))
    comb = comb / jnp.sum(comb, axis=0, keepdims=True)
    probs[0, 0] = disp
    probs[0, 1] = comb
    first = pl.multiple_of(image * SLOTS, SLOTS)
    rows[pl.ds(first, SLOTS), :] = mm(disp.astype(BF16), tok).astype(BF16)
    rows[pl.ds(64 + first, SLOTS), :] = mm(comb.astype(BF16), cotangent[0]).astype(BF16)

    @pl.when(image == 1)
    def _():
        message[...] = to_message(core[0], rows[...])


def route(core, tokens, router, cotangent):
    image = pl.BlockSpec((1, M, D), lambda b: (b, 0, 0))
    probs = pl.BlockSpec((1, 2, SLOTS, M), lambda b: (b, 0, 0, 0))
    return pl.pallas_call(
        route_kernel,
        grid=(2,),
        in_specs=[SMEM, image, pl.BlockSpec((SLOTS, D), lambda b: (0, 0)), image],
        out_specs=[pl.BlockSpec((128, D), lambda b: (0, 0)), probs],
        out_shape=[
            jax.ShapeDtypeStruct((128, D), BF16),
            jax.ShapeDtypeStruct((2, 2, SLOTS, M), F32),
        ],
        scratch_shapes=[pltpu.VMEM((128, D), BF16)],
        compiler_params=pltpu.CompilerParams(vmem_limit_bytes=56 * 2**20),
        cost_estimate=cost(10**9, 3 * 10**6),
    )(core, tokens, router, cotangent)


def experts_kernel(n, *refs):
    held, (w_in, w_out) = refs[:n], refs[n : n + 2]
    sent, (hidden, grad_preact) = refs[n + 2 : 2 * n + 2], refs[2 * n + 2 :]
    rows = jnp.concatenate([h[:, :D] for h in held], axis=0)
    grad_rows = jnp.concatenate([h[:, D:] for h in held], axis=0)
    x = mm(rows, w_in[...])
    square = x * x
    scale = 0.7978845608028654
    t = jnp.tanh(scale * (x + 0.044715 * (square * x)))
    half = 0.5 * (1.0 + t)
    hid = (x * half).astype(BF16)
    slope = half + 0.5 * x * (1.0 - t * t) * (scale * (1.0 + 0.134145 * square))
    hidden[...] = hid
    grad = (mm_nt(grad_rows, w_out[...]) * slope).astype(BF16)
    grad_preact[...] = grad
    out = mm(hid, w_out[...]).astype(BF16)
    inner = mm_nt(grad, w_in[...]).astype(BF16)
    first = 0
    for s in sent:
        last = first + s.shape[0]
        s[:, :D] = out[first:last]
        s[:, D:] = inner[first:last]
        first = last


def experts(held, w_in, w_out):
    n = len(held)
    total = sum(h.shape[0] for h in held)
    shapes = [jax.ShapeDtypeStruct(h.shape, BF16) for h in held]
    shapes += [jax.ShapeDtypeStruct((total, HID), BF16)] * 2
    results = pl.pallas_call(
        functools.partial(experts_kernel, n),
        in_specs=[VMEM] * (n + 2),
        out_specs=[VMEM] * (n + 2),
        out_shape=shapes,
        compiler_params=PARAMS,
        cost_estimate=cost(8 * total * D * HID, 4 * 10**6),
    )(*held, w_in, w_out)
    return results[:n], results[n], results[n + 1]


def pack_kernel(stay, go, message):
    rows = jnp.concatenate([stay[:, :D], stay[:, D:], go[:, :D], go[:, D:]], axis=0)
    r = lax.broadcasted_iota(jnp.int32, (128, 128), 0)
    n = lax.broadcasted_iota(jnp.int32, (128, 128), 1)
    pick = n == ((r >> 2) & 1) * 64 + ((r >> 1) & 1) * 32 + (r >> 3) * 2 + (r & 1)
    message[...] = mm(pick.astype(F32).astype(BF16), rows).astype(BF16)


def pack(stay, go):
    return pl.pallas_call(
        pack_kernel,
        in_specs=[VMEM] * 2,
        out_specs=VMEM,
        out_shape=jax.ShapeDtypeStruct((128, D), BF16),
        compiler_params=PARAMS,
        cost_estimate=cost(10**8, 10**6),
    )(stay, go)


def gate_kernel(core, message, tokens, cotangent, probs, slots, gates, term):
    rows = from_message(core[0], message[...])
    slots[...] = rows
    total = jnp.zeros((SLOTS, D), F32)
    for b in range(2):
        disp, comb = probs[b, 0], probs[b, 1]
        grad_comb = mm_nt(rows[b * 32 : b * 32 + 32], cotangent[b])
        grad_disp = mm_nt(rows[64 + b * 32 : 96 + b * 32], tokens[b])
        grad = comb * (grad_comb - jnp.sum(comb * grad_comb, axis=0, keepdims=True))
        grad += disp * (grad_disp - jnp.sum(disp * grad_disp, axis=1, keepdims=True))
        grad = grad.astype(BF16)
        gates[b] = grad
        total += mm(grad, tokens[b])
    total = total.astype(BF16)
    for e in range(16):
        term[e] = total[2 * e : 2 * e + 2]


def gate(core, message, tokens, cotangent, probs):
    return pl.pallas_call(
        gate_kernel,
        in_specs=[SMEM] + [VMEM] * 4,
        out_specs=[VMEM] * 3,
        out_shape=[
            jax.ShapeDtypeStruct((128, D), BF16),
            jax.ShapeDtypeStruct((2, SLOTS, M), BF16),
            jax.ShapeDtypeStruct((16, 2, D), BF16),
        ],
        compiler_params=PARAMS,
        cost_estimate=cost(10**9, 3 * 10**6),
    )(core, message, tokens, cotangent, probs)


def spread_kernel(slots, gates, probs, router, output, grad_tokens):
    first = pl.multiple_of(pl.program_id(0) * SLOTS, SLOTS)
    slots_out = slots[pl.ds(first, SLOTS), :]
    grad_slots_in = slots[pl.ds(64 + first, SLOTS), :]
    output[0] = mm_tn(probs[0, 1].astype(BF16), slots_out).astype(BF16)
    grad = mm_tn(probs[0, 0].astype(BF16), grad_slots_in) + mm_tn(gates[0], router[...])
    grad_tokens[0] = grad.astype(BF16)


def spread(slots, gates, probs, router):
    image = pl.BlockSpec((1, M, D), lambda b: (b, 0, 0))
    shares = pl.BlockSpec((1, 2, SLOTS, M), lambda b: (b, 0, 0, 0))
    return pl.pallas_call(
        spread_kernel,
        grid=(2,),
        in_specs=[
            pl.BlockSpec((128, D), lambda b: (0, 0)),
            pl.BlockSpec((1, SLOTS, M), lambda b: (b, 0, 0)),
            shares,
            pl.BlockSpec((SLOTS, D), lambda b: (0, 0)),
        ],
        out_specs=[image, image],
        out_shape=[jax.ShapeDtypeStruct((2, M, D), BF16)] * 2,
        compiler_params=PARAMS,
        cost_estimate=cost(10**9, 3 * 10**6),
    )(slots, gates, probs, router)


def low(a):
    return a[:32]


def high(a):
    return a[32:]


def join(a, b):
    return jnp.concatenate([a, b])


def sum_over_all(term):
    part = exchange(term, PLANE)
    part = jnp.sum(part.astype(F32), axis=0).astype(BF16)
    part = exchange(jnp.broadcast_to(part[None], (16, 2, D)), COLUMN)
    part = jnp.sum(part.astype(F32), axis=0).astype(BF16)
    part = exchange(jnp.broadcast_to(part[None], (16, 2, D)), PLANE)
    return part.reshape(SLOTS, D).astype(F32)


def shards(tokens, router, w_in, w_out, cotangent):
    core = lax.axis_index("c").astype(jnp.int32).reshape(1)
    w_in, w_out = w_in[0], w_out[0]
    message, probs = route(core, tokens, router, cotangent)

    arrived = exchange(message.reshape(16, 8, D), COLUMN)
    arrived = arrived.reshape(16, 2, 2, 2, D).transpose(1, 0, 3, 2, 4).reshape(2, 32, 2 * D)
    own = join(arrived[0], core_swap(arrived[1]))

    down, up, side = x_up(own), x_down(own), y_swap(own)
    first = x_up(join(low(side), low(down)))
    second = x_down(join(low(side), high(up)))
    third = y_swap(join(high(down), high(up)))
    near = experts((own, down, up, side), w_in, w_out)
    first, third, near = lax.optimization_barrier((first, third, near))
    far_low = x_up(low(first))
    far_high = x_down(high(third))
    middle = experts((first, second, third), w_in, w_out)
    far_low, far_high, middle = lax.optimization_barrier((far_low, far_high, middle))
    far = experts((far_low, far_high), w_in, w_out)

    (own_sum, down_sum, up_sum, side_sum), (first_sum, second_sum, third_sum) = near[0], middle[0]
    low_sum, high_sum = far[0]
    low_in, high_in = x_down(low_sum), x_up(high_sum)
    second_in = x_up(second_sum)
    first_in = x_down(join(add(low(first_sum), low_in), high(first_sum)))
    third_in = y_swap(join(low(third_sum), add(high(third_sum), high_in)))
    side_in = y_swap(join(add(low(side_sum), low(first_in), low(second_in)), high(side_sum)))
    down_in = x_down(
        join(add(low(down_sum), high(first_in)), add(high(down_sum), low(third_in)))
    )
    up_in = x_up(join(low(up_sum), add(high(up_sum), high(second_in), high(third_in))))
    summed = add(own_sum, down_in, up_in, side_in)

    leaving = pack(low(summed), core_swap(high(summed)))
    returned = exchange(leaving.reshape(16, 8, D), COLUMN).reshape(128, D)
    slots, gates, term = gate(core, returned, tokens, cotangent, probs)
    grad_router = sum_over_all(term)
    output, grad_tokens = spread(slots, gates, probs, router)

    rows = jnp.concatenate([own, down, up, side, first, second, third, far_low, far_high])
    hidden = jnp.concatenate([near[1], middle[1], far[1]])
    grad_preact = jnp.concatenate([near[2], middle[2], far[2]])
    grad_in = mm_tn(rows[:, :D], grad_preact).astype(BF16)
    grad_out = mm_tn(hidden, rows[:, D:]).astype(BF16)
    return (output, grad_tokens, grad_router, grad_in[None], grad_out[None])


def solution(mesh):
    fine = Mesh(mesh.devices.reshape(2, 4, 2, 8, 2), AXES)
    images = P(AXES, None, None)
    placed = (images, P(), P(EXPERT, None, DP), P(EXPERT, DP, None), images)
    return jax.shard_map(
        shards,
        mesh=fine,
        in_specs=placed,
        out_specs=(images, images, P(), placed[2], placed[3]),
        check_vma=False,
    )
```

```python
import functools

import jax
import jax.numpy as jnp
from jax import lax
from jax.experimental import pallas as pl
from jax.experimental.pallas import tpu as pltpu
from jax.sharding import Mesh, PartitionSpec as P

BF16 = jnp.bfloat16
F32 = jnp.float32
D = 1280
M = 256
SLOTS = 32
HID = 640
AXES = ("yl", "x", "yh", "z", "c")
DP = ("yl", "x")
EXPERT = ("yh", "z", "c")
PLANE = ("yl", "x", "c")
COLUMN = ("yh", "z")
VMEM = pl.BlockSpec(memory_space=pltpu.VMEM)
SMEM = pl.BlockSpec(memory_space=pltpu.SMEM)
PARAMS = pltpu.CompilerParams(vmem_limit_bytes=16 * 2**20)


def cost(flops, size):
    return pl.CostEstimate(flops=flops, bytes_accessed=size, transcendentals=0)


def mm(a, b):
    return jnp.dot(a, b, preferred_element_type=F32)


def mm_nt(a, b):
    return lax.dot_general(a, b, (((1,), (1,)), ((), ())), preferred_element_type=F32)


def mm_tn(a, b):
    return lax.dot_general(a, b, (((0,), (0,)), ((), ())), preferred_element_type=F32)


def add(*terms):
    total = terms[0].astype(F32)
    for term in terms[1:]:
        total = total + term.astype(F32)
    return total.astype(BF16)


def exchange(x, axes):
    return lax.all_to_all(x, axes, split_axis=0, concat_axis=0, tiled=True)


def x_up(a):
    return lax.ppermute(a, "x", [(i, (i + 1) % 4) for i in range(4)])


def x_down(a):
    return lax.ppermute(a, "x", [(i, (i + 3) % 4) for i in range(4)])


def y_swap(a):
    return lax.ppermute(a, "yl", [(0, 1), (1, 0)])


def core_swap(a):
    return lax.ppermute(a, "c", [(0, 1), (1, 0)])


def natural_row(r, core):
    slot = 2 * (r >> 3) + (((r >> 2) & 1) ^ core)
    return ((r >> 1) & 1) * 64 + (r & 1) * 32 + slot


def to_message(core, rows):
    r = lax.broadcasted_iota(jnp.int32, (128, 128), 0)
    n = lax.broadcasted_iota(jnp.int32, (128, 128), 1)
    pick = (n == natural_row(r, core)).astype(F32).astype(BF16)
    return mm(pick, rows).astype(BF16)


def from_message(core, message):
    n = lax.broadcasted_iota(jnp.int32, (128, 128), 0)
    r = lax.broadcasted_iota(jnp.int32, (128, 128), 1)
    pick = (n == natural_row(r, core)).astype(F32).astype(BF16)
    return mm(pick, message).astype(BF16)


def route_kernel(core, tokens, router, cotangent, message, probs, rows):
    image = pl.program_id(0)
    tok = tokens[0]
    logits = mm_nt(router[...], tok)
    disp = jnp.exp(logits - jnp.max(logits, axis=1, keepdims=True))
    disp = disp / jnp.sum(disp, axis=1, keepdims=True)
    comb = jnp.exp(logits - jnp.max(logits, axis=0, keepdims=True))
    comb = comb / jnp.sum(comb, axis=0, keepdims=True)
    probs[0, 0] = disp
    probs[0, 1] = comb
    first = pl.multiple_of(image * SLOTS, SLOTS)
    rows[pl.ds(first, SLOTS), :] = mm(disp.astype(BF16), tok).astype(BF16)
    rows[pl.ds(64 + first, SLOTS), :] = mm(comb.astype(BF16), cotangent[0]).astype(BF16)

    @pl.when(image == 1)
    def _():
        message[...] = to_message(core[0], rows[...])


def route(core, tokens, router, cotangent):
    image = pl.BlockSpec((1, M, D), lambda b: (b, 0, 0))
    probs = pl.BlockSpec((1, 2, SLOTS, M), lambda b: (b, 0, 0, 0))
    return pl.pallas_call(
        route_kernel,
        grid=(2,),
        in_specs=[SMEM, image, pl.BlockSpec((SLOTS, D), lambda b: (0, 0)), image],
        out_specs=[pl.BlockSpec((128, D), lambda b: (0, 0)), probs],
        out_shape=[
            jax.ShapeDtypeStruct((128, D), BF16),
            jax.ShapeDtypeStruct((2, 2, SLOTS, M), F32),
        ],
        scratch_shapes=[pltpu.VMEM((128, D), BF16)],
        compiler_params=pltpu.CompilerParams(vmem_limit_bytes=56 * 2**20),
        cost_estimate=cost(10**9, 3 * 10**6),
    )(core, tokens, router, cotangent)


def experts_kernel(n, order, *refs):
    held, (w_in, w_out) = refs[:n], refs[n : n + 2]
    sent, (hidden, grad_preact) = refs[n + 2 : 2 * n + 2], refs[2 * n + 2 :]
    rows = jnp.concatenate([h[:, :D] for h in held], axis=0)
    grad_rows = jnp.concatenate([h[:, D:] for h in held], axis=0)
    x = mm(rows, w_in[...])
    square = x * x
    scale = 0.7978845608028654
    t = jnp.tanh(scale * (x + 0.044715 * (square * x)))
    half = 0.5 * (1.0 + t)
    hid = (x * half).astype(BF16)
    slope = half + 0.5 * x * (1.0 - t * t) * (scale * (1.0 + 0.134145 * square))
    hidden[...] = hid
    grad = (mm_nt(grad_rows, w_out[...]) * slope).astype(BF16)
    grad_preact[...] = grad
    out = mm(hid, w_out[...]).astype(BF16)
    inner = mm_nt(grad, w_in[...]).astype(BF16)
    first = 0
    for s in sent:
        for at in range(0, s.shape[0], 32):
            block = order[first] * 32
            s[at : at + 32, :D] = out[block : block + 32]
            s[at : at + 32, D:] = inner[block : block + 32]
            first += 1


def experts(held, w_in, w_out, order=None):
    n = len(held)
    total = sum(h.shape[0] for h in held)
    order = order or tuple(range(total // 32))
    shapes = [jax.ShapeDtypeStruct(h.shape, BF16) for h in held]
    shapes += [jax.ShapeDtypeStruct((total, HID), BF16)] * 2
    results = pl.pallas_call(
        functools.partial(experts_kernel, n, order),
        in_specs=[VMEM] * (n + 2),
        out_specs=[VMEM] * (n + 2),
        out_shape=shapes,
        compiler_params=PARAMS,
        cost_estimate=cost(8 * total * D * HID, 4 * 10**6),
    )(*held, w_in, w_out)
    return results[:n], results[n], results[n + 1]


def pack_kernel(stay, go, message):
    rows = jnp.concatenate([stay[:, :D], stay[:, D:], go[:, :D], go[:, D:]], axis=0)
    r = lax.broadcasted_iota(jnp.int32, (128, 128), 0)
    n = lax.broadcasted_iota(jnp.int32, (128, 128), 1)
    pick = n == ((r >> 2) & 1) * 64 + ((r >> 1) & 1) * 32 + (r >> 3) * 2 + (r & 1)
    message[...] = mm(pick.astype(F32).astype(BF16), rows).astype(BF16)


def pack(stay, go):
    return pl.pallas_call(
        pack_kernel,
        in_specs=[VMEM] * 2,
        out_specs=VMEM,
        out_shape=jax.ShapeDtypeStruct((128, D), BF16),
        compiler_params=PARAMS,
        cost_estimate=cost(10**8, 10**6),
    )(stay, go)


def hold_kernel(probs, out):
    out[...] = probs[...]


def hold(probs):
    return pl.pallas_call(
        hold_kernel,
        in_specs=[VMEM],
        out_specs=VMEM,
        out_shape=jax.ShapeDtypeStruct(probs.shape, F32),
        compiler_params=PARAMS,
        cost_estimate=cost(10**6, 10**6),
    )(probs)


def gate_kernel(core, message, tokens, cotangent, probs, gates, term):
    rows = from_message(core[0], message[...])
    total = jnp.zeros((SLOTS, D), F32)
    for b in range(2):
        disp, comb = probs[b, 0], probs[b, 1]
        grad_comb = mm_nt(rows[b * 32 : b * 32 + 32], cotangent[b])
        grad_disp = mm_nt(rows[64 + b * 32 : 96 + b * 32], tokens[b])
        grad = comb * (grad_comb - jnp.sum(comb * grad_comb, axis=0, keepdims=True))
        grad += disp * (grad_disp - jnp.sum(disp * grad_disp, axis=1, keepdims=True))
        grad = grad.astype(BF16)
        gates[b] = grad
        total += mm(grad, tokens[b])
    total = total.astype(BF16)
    for e in range(16):
        term[e] = total[2 * e : 2 * e + 2]


def gate(core, message, tokens, cotangent, probs):
    return pl.pallas_call(
        gate_kernel,
        in_specs=[SMEM] + [VMEM] * 4,
        out_specs=[VMEM] * 2,
        out_shape=[
            jax.ShapeDtypeStruct((2, SLOTS, M), BF16),
            jax.ShapeDtypeStruct((16, 2, D), BF16),
        ],
        compiler_params=PARAMS,
        cost_estimate=cost(10**9, 3 * 10**6),
    )(core, message, tokens, cotangent, probs)


def spread_kernel(core, message, gates, probs, router, output, grad_tokens, rows):
    image = pl.program_id(0)

    @pl.when(image == 0)
    def _():
        rows[...] = from_message(core[0], message[...])

    first = pl.multiple_of(image * SLOTS, SLOTS)
    slots_out = rows[pl.ds(first, SLOTS), :]
    grad_slots_in = rows[pl.ds(64 + first, SLOTS), :]
    output[0] = mm_tn(probs[0, 1].astype(BF16), slots_out).astype(BF16)
    grad = mm_tn(probs[0, 0].astype(BF16), grad_slots_in) + mm_tn(gates[0], router[...])
    grad_tokens[0] = grad.astype(BF16)


def spread(core, message, gates, probs, router):
    image = pl.BlockSpec((1, M, D), lambda b: (b, 0, 0))
    return pl.pallas_call(
        spread_kernel,
        grid=(2,),
        in_specs=[
            SMEM,
            pl.BlockSpec((128, D), lambda b: (0, 0)),
            pl.BlockSpec((1, SLOTS, M), lambda b: (b, 0, 0)),
            pl.BlockSpec((1, 2, SLOTS, M), lambda b: (b, 0, 0, 0)),
            pl.BlockSpec((SLOTS, D), lambda b: (0, 0)),
        ],
        out_specs=[image, image],
        out_shape=[jax.ShapeDtypeStruct((2, M, D), BF16)] * 2,
        scratch_shapes=[pltpu.VMEM((128, D), BF16)],
        compiler_params=PARAMS,
        cost_estimate=cost(10**9, 3 * 10**6),
    )(core, message, gates, probs, router)


def low(a):
    return a[:32]


def high(a):
    return a[32:]


def join(a, b):
    return jnp.concatenate([a, b])


def sum_over_all(term):
    part = exchange(term, PLANE)
    part = jnp.sum(part.astype(F32), axis=0).astype(BF16)
    part = exchange(jnp.broadcast_to(part[None], (16, 2, D)), COLUMN)
    part = jnp.sum(part.astype(F32), axis=0).astype(BF16)
    part = exchange(jnp.broadcast_to(part[None], (16, 2, D)), PLANE)
    return part.reshape(SLOTS, D).astype(F32)


def shards(tokens, router, w_in, w_out, cotangent):
    core = lax.axis_index("c").astype(jnp.int32).reshape(1)
    w_in, w_out = w_in[0], w_out[0]
    message, probs = route(core, tokens, router, cotangent)

    arrived = exchange(message.reshape(16, 8, D), COLUMN)
    arrived = arrived.reshape(16, 2, 2, 2, D).transpose(1, 0, 3, 2, 4).reshape(2, 32, 2 * D)
    own = join(arrived[0], core_swap(arrived[1]))

    down, up, side = x_up(own), x_down(own), y_swap(own)
    first = x_up(join(low(side), low(down)))
    third = y_swap(join(high(down), high(up)))
    near = experts((own, down, up, side), w_in, w_out)
    late, near = lax.optimization_barrier((join(low(side), high(up)), near))
    second = x_down(late)
    far_low = x_up(low(first))
    far_high = x_down(high(third))
    far = experts((far_low, far_high), w_in, w_out)
    first, far = lax.optimization_barrier((first, far))
    middle = experts((first, second, third), w_in, w_out, (0, 1, 5, 3, 4, 2))

    (own_sum, down_sum, up_sum, side_sum), (first_sum, second_sum, third_sum) = near[0], middle[0]
    low_sum, high_sum = far[0]
    low_in, high_in, third_in = x_down(low_sum), x_up(high_sum), y_swap(third_sum)
    first_in = x_down(join(add(low(first_sum), low_in), high(first_sum)))
    second_in = x_up(join(add(low(second_sum), high_in), high(second_sum)))
    down_in = x_down(
        join(add(low(down_sum), high(first_in)), add(high(down_sum), low(third_in)))
    )
    up_in = x_up(
        join(add(low(up_sum), high(third_in)), add(high(up_sum), high(second_in)))
    )
    side_in = y_swap(
        join(add(low(side_sum), low(first_in)), add(high(side_sum), low(second_in)))
    )
    summed = add(own_sum, down_in, up_in, side_in)

    leaving = pack(low(summed), core_swap(high(summed)))
    leaving, probs = lax.optimization_barrier((leaving, probs))
    probs = hold(probs)
    returned = exchange(leaving.reshape(16, 8, D), COLUMN).reshape(128, D)
    gates, term = gate(core, returned, tokens, cotangent, probs)
    grad_router = sum_over_all(term)
    output, grad_tokens = spread(core, returned, gates, probs, router)

    rows = jnp.concatenate([own, down, up, side, first, second, third, far_low, far_high])
    hidden = jnp.concatenate([near[1], middle[1], far[1]])
    grad_preact = jnp.concatenate([near[2], middle[2], far[2]])
    grad_in = mm_tn(rows[:, :D], grad_preact).astype(BF16)
    grad_out = mm_tn(hidden, rows[:, D:]).astype(BF16)
    return (output, grad_tokens, grad_router, grad_in[None], grad_out[None])


def solution(mesh):
    fine = Mesh(mesh.devices.reshape(2, 4, 2, 8, 2), AXES)
    images = P(AXES, None, None)
    placed = (images, P(), P(EXPERT, None, DP), P(EXPERT, DP, None), images)
    return jax.shard_map(
        shards,
        mesh=fine,
        in_specs=placed,
        out_specs=(images, images, P(), placed[2], placed[3]),
        check_vma=False,
    )
```

```python
import functools

import jax
import jax.numpy as jnp
from jax import lax
from jax.experimental import pallas as pl
from jax.experimental.pallas import tpu as pltpu
from jax.sharding import Mesh, PartitionSpec as P

BF16 = jnp.bfloat16
F32 = jnp.float32
D = 1280
M = 256
SLOTS = 32
HID = 640
AXES = ("yl", "x", "yh", "z", "c")
DP = ("yl", "x")
EXPERT = ("yh", "z", "c")
PLANE = ("yl", "x", "c")
COLUMN = ("yh", "z")
VMEM = pl.BlockSpec(memory_space=pltpu.VMEM)
SMEM = pl.BlockSpec(memory_space=pltpu.SMEM)
PARAMS = pltpu.CompilerParams(vmem_limit_bytes=16 * 2**20)


def cost(flops, size):
    return pl.CostEstimate(flops=flops, bytes_accessed=size, transcendentals=0)


def mm(a, b):
    return jnp.dot(a, b, preferred_element_type=F32)


def mm_nt(a, b):
    return lax.dot_general(a, b, (((1,), (1,)), ((), ())), preferred_element_type=F32)


def mm_tn(a, b):
    return lax.dot_general(a, b, (((0,), (0,)), ((), ())), preferred_element_type=F32)


def add(*terms):
    total = terms[0].astype(F32)
    for term in terms[1:]:
        total = total + term.astype(F32)
    return total.astype(BF16)


def exchange(x, axes):
    return lax.all_to_all(x, axes, split_axis=0, concat_axis=0, tiled=True)


def x_up(a):
    return lax.ppermute(a, "x", [(i, (i + 1) % 4) for i in range(4)])


def x_down(a):
    return lax.ppermute(a, "x", [(i, (i + 3) % 4) for i in range(4)])


def y_swap(a):
    return lax.ppermute(a, "yl", [(0, 1), (1, 0)])


def core_swap(a):
    return lax.ppermute(a, "c", [(0, 1), (1, 0)])


def natural_row(r, core):
    slot = 2 * (r >> 3) + (((r >> 2) & 1) ^ core)
    return ((r >> 1) & 1) * 64 + (r & 1) * 32 + slot


def to_message(core, rows):
    r = lax.broadcasted_iota(jnp.int32, (128, 128), 0)
    n = lax.broadcasted_iota(jnp.int32, (128, 128), 1)
    pick = (n == natural_row(r, core)).astype(F32).astype(BF16)
    return mm(pick, rows).astype(BF16)


def from_message(core, message):
    n = lax.broadcasted_iota(jnp.int32, (128, 128), 0)
    r = lax.broadcasted_iota(jnp.int32, (128, 128), 1)
    pick = (n == natural_row(r, core)).astype(F32).astype(BF16)
    return mm(pick, message).astype(BF16)


def route_kernel(core, tokens, router, cotangent, message, probs, rows):
    image = pl.program_id(0)
    tok = tokens[0]
    logits = mm_nt(router[...], tok)
    disp = jnp.exp(logits - jnp.max(logits, axis=1, keepdims=True))
    disp = disp / jnp.sum(disp, axis=1, keepdims=True)
    comb = jnp.exp(logits - jnp.max(logits, axis=0, keepdims=True))
    comb = comb / jnp.sum(comb, axis=0, keepdims=True)
    probs[0, 0] = disp
    probs[0, 1] = comb
    first = pl.multiple_of(image * SLOTS, SLOTS)
    rows[pl.ds(first, SLOTS), :] = mm(disp.astype(BF16), tok).astype(BF16)
    rows[pl.ds(64 + first, SLOTS), :] = mm(comb.astype(BF16), cotangent[0]).astype(BF16)

    @pl.when(image == 1)
    def _():
        message[...] = to_message(core[0], rows[...])


def route(core, tokens, router, cotangent):
    image = pl.BlockSpec((1, M, D), lambda b: (b, 0, 0))
    probs = pl.BlockSpec((1, 2, SLOTS, M), lambda b: (b, 0, 0, 0))
    return pl.pallas_call(
        route_kernel,
        grid=(2,),
        in_specs=[SMEM, image, pl.BlockSpec((SLOTS, D), lambda b: (0, 0)), image],
        out_specs=[pl.BlockSpec((128, D), lambda b: (0, 0)), probs],
        out_shape=[
            jax.ShapeDtypeStruct((128, D), BF16),
            jax.ShapeDtypeStruct((2, 2, SLOTS, M), F32),
        ],
        scratch_shapes=[pltpu.VMEM((128, D), BF16)],
        compiler_params=pltpu.CompilerParams(vmem_limit_bytes=56 * 2**20),
        cost_estimate=cost(10**9, 3 * 10**6),
    )(core, tokens, router, cotangent)


def experts_kernel(n, order, *refs):
    held, (w_in, w_out) = refs[:n], refs[n : n + 2]
    sent, (hidden, grad_preact) = refs[n + 2 : 2 * n + 2], refs[2 * n + 2 :]
    rows = jnp.concatenate([h[:, :D] for h in held], axis=0)
    grad_rows = jnp.concatenate([h[:, D:] for h in held], axis=0)
    x = mm(rows, w_in[...])
    square = x * x
    scale = 0.7978845608028654
    t = jnp.tanh(scale * (x + 0.044715 * (square * x)))
    half = 0.5 * (1.0 + t)
    hid = (x * half).astype(BF16)
    slope = half + 0.5 * x * (1.0 - t * t) * (scale * (1.0 + 0.134145 * square))
    hidden[...] = hid
    grad = (mm_nt(grad_rows, w_out[...]) * slope).astype(BF16)
    grad_preact[...] = grad
    out = mm(hid, w_out[...]).astype(BF16)
    inner = mm_nt(grad, w_in[...]).astype(BF16)
    first = 0
    for s in sent:
        for at in range(0, s.shape[0], 32):
            block = order[first] * 32
            s[at : at + 32, :D] = out[block : block + 32]
            s[at : at + 32, D:] = inner[block : block + 32]
            first += 1


def experts(held, w_in, w_out, order=None):
    n = len(held)
    total = sum(h.shape[0] for h in held)
    order = order or tuple(range(total // 32))
    shapes = [jax.ShapeDtypeStruct(h.shape, BF16) for h in held]
    shapes += [jax.ShapeDtypeStruct((total, HID), BF16)] * 2
    results = pl.pallas_call(
        functools.partial(experts_kernel, n, order),
        in_specs=[VMEM] * (n + 2),
        out_specs=[VMEM] * (n + 2),
        out_shape=shapes,
        compiler_params=PARAMS,
        cost_estimate=cost(8 * total * D * HID, 4 * 10**6),
    )(*held, w_in, w_out)
    return results[:n], results[n], results[n + 1]


def grads_kernel(n, m, *refs):
    pieces, acts, (grad_in, grad_out) = refs[:n], refs[n : n + 2 * m], refs[n + 2 * m :]
    rows = jnp.concatenate([p[:, :D] for p in pieces], axis=0)
    grad_preact = jnp.concatenate([a[...] for a in acts[m:]], axis=0)
    grad_in[...] = mm_tn(rows, grad_preact).astype(BF16)
    hidden = jnp.concatenate([a[...] for a in acts[:m]], axis=0)
    grad_rows = jnp.concatenate([p[:, D:] for p in pieces], axis=0)
    grad_out[...] = mm_tn(hidden, grad_rows).astype(BF16)


def weight_grads(pieces, hidden, grad_preact):
    n, m = len(pieces), len(hidden)
    return pl.pallas_call(
        functools.partial(grads_kernel, n, m),
        in_specs=[VMEM] * (n + 2 * m),
        out_specs=[VMEM] * 2,
        out_shape=[
            jax.ShapeDtypeStruct((D, HID), BF16),
            jax.ShapeDtypeStruct((HID, D), BF16),
        ],
        compiler_params=PARAMS,
        cost_estimate=cost(4 * 512 * D * HID, 8 * 10**6),
    )(*pieces, *hidden, *grad_preact)


def pack_kernel(stay, go, message):
    rows = jnp.concatenate([stay[:, :D], stay[:, D:], go[:, :D], go[:, D:]], axis=0)
    r = lax.broadcasted_iota(jnp.int32, (128, 128), 0)
    n = lax.broadcasted_iota(jnp.int32, (128, 128), 1)
    pick = n == ((r >> 2) & 1) * 64 + ((r >> 1) & 1) * 32 + (r >> 3) * 2 + (r & 1)
    message[...] = mm(pick.astype(F32).astype(BF16), rows).astype(BF16)


def pack(stay, go):
    return pl.pallas_call(
        pack_kernel,
        in_specs=[VMEM] * 2,
        out_specs=VMEM,
        out_shape=jax.ShapeDtypeStruct((128, D), BF16),
        compiler_params=PARAMS,
        cost_estimate=cost(10**8, 10**6),
    )(stay, go)


def hold_kernel(probs, out):
    out[...] = probs[...]


def hold(probs):
    return pl.pallas_call(
        hold_kernel,
        in_specs=[VMEM],
        out_specs=VMEM,
        out_shape=jax.ShapeDtypeStruct(probs.shape, F32),
        compiler_params=PARAMS,
        cost_estimate=cost(10**6, 10**6),
    )(probs)


def hold_inputs_kernel(tokens, cotangent, tokens_out, cotangent_out):
    tokens_out[...] = tokens[...]
    cotangent_out[...] = cotangent[...]


def hold_inputs(tokens, cotangent):
    return pl.pallas_call(
        hold_inputs_kernel,
        in_specs=[VMEM] * 2,
        out_specs=[VMEM] * 2,
        out_shape=[jax.ShapeDtypeStruct((2, M, D), BF16)] * 2,
        compiler_params=PARAMS,
        cost_estimate=cost(10**6, 5 * 10**6),
    )(tokens, cotangent)


def gate_kernel(core, message, tokens, cotangent, probs, gates, term):
    rows = from_message(core[0], message[...])
    total = jnp.zeros((SLOTS, D), F32)
    for b in range(2):
        disp, comb = probs[b, 0], probs[b, 1]
        grad_comb = mm_nt(rows[b * 32 : b * 32 + 32], cotangent[b])
        grad_disp = mm_nt(rows[64 + b * 32 : 96 + b * 32], tokens[b])
        grad = comb * (grad_comb - jnp.sum(comb * grad_comb, axis=0, keepdims=True))
        grad += disp * (grad_disp - jnp.sum(disp * grad_disp, axis=1, keepdims=True))
        grad = grad.astype(BF16)
        gates[b] = grad
        total += mm(grad, tokens[b])
    total = total.astype(BF16)
    for e in range(16):
        term[e] = total[2 * e : 2 * e + 2]


def gate(core, message, tokens, cotangent, probs):
    return pl.pallas_call(
        gate_kernel,
        in_specs=[SMEM] + [VMEM] * 4,
        out_specs=[VMEM] * 2,
        out_shape=[
            jax.ShapeDtypeStruct((2, SLOTS, M), BF16),
            jax.ShapeDtypeStruct((16, 2, D), BF16),
        ],
        compiler_params=PARAMS,
        cost_estimate=cost(10**9, 3 * 10**6),
    )(core, message, tokens, cotangent, probs)


def spread_kernel(core, message, gates, probs, router, output, grad_tokens, rows):
    image = pl.program_id(0)

    @pl.when(image == 0)
    def _():
        rows[...] = from_message(core[0], message[...])

    first = pl.multiple_of(image * SLOTS, SLOTS)
    slots_out = rows[pl.ds(first, SLOTS), :]
    grad_slots_in = rows[pl.ds(64 + first, SLOTS), :]
    output[0] = mm_tn(probs[0, 1].astype(BF16), slots_out).astype(BF16)
    grad = mm_tn(probs[0, 0].astype(BF16), grad_slots_in) + mm_tn(gates[0], router[...])
    grad_tokens[0] = grad.astype(BF16)


def spread(core, message, gates, probs, router):
    image = pl.BlockSpec((1, M, D), lambda b: (b, 0, 0))
    return pl.pallas_call(
        spread_kernel,
        grid=(2,),
        in_specs=[
            SMEM,
            pl.BlockSpec((128, D), lambda b: (0, 0)),
            pl.BlockSpec((1, SLOTS, M), lambda b: (b, 0, 0)),
            pl.BlockSpec((1, 2, SLOTS, M), lambda b: (b, 0, 0, 0)),
            pl.BlockSpec((SLOTS, D), lambda b: (0, 0)),
        ],
        out_specs=[image, image],
        out_shape=[jax.ShapeDtypeStruct((2, M, D), BF16)] * 2,
        scratch_shapes=[pltpu.VMEM((128, D), BF16)],
        compiler_params=PARAMS,
        cost_estimate=cost(10**9, 3 * 10**6),
    )(core, message, gates, probs, router)


def low(a):
    return a[:32]


def high(a):
    return a[32:]


def join(a, b):
    return jnp.concatenate([a, b])


def sum_over_all(term):
    part = exchange(term, PLANE)
    part = jnp.sum(part.astype(F32), axis=0).astype(BF16)
    part = exchange(jnp.broadcast_to(part[None], (16, 2, D)), COLUMN)
    part = jnp.sum(part.astype(F32), axis=0).astype(BF16)
    part = exchange(jnp.broadcast_to(part[None], (16, 2, D)), PLANE)
    return part.reshape(SLOTS, D).astype(F32)


def shards(tokens, router, w_in, w_out, cotangent):
    core = lax.axis_index("c").astype(jnp.int32).reshape(1)
    w_in, w_out = w_in[0], w_out[0]
    message, probs = route(core, tokens, router, cotangent)

    arrived = exchange(message.reshape(16, 8, D), COLUMN)
    arrived = arrived.reshape(16, 2, 2, 2, D).transpose(1, 0, 3, 2, 4).reshape(2, 32, 2 * D)
    own = join(arrived[0], core_swap(arrived[1]))

    down, up, side = x_up(own), x_down(own), y_swap(own)
    first = x_up(join(low(side), low(down)))
    third = y_swap(join(high(down), high(up)))
    near = experts((own, down, up, side), w_in, w_out)
    late, near = lax.optimization_barrier((join(low(side), high(up)), near))
    second = x_down(late)
    far_low = x_up(low(first))
    far_high = x_down(high(third))
    far = experts((far_low, far_high), w_in, w_out)
    first, far = lax.optimization_barrier((first, far))
    middle = experts((first, second, third), w_in, w_out, (0, 1, 5, 3, 4, 2))

    (own_sum, down_sum, up_sum, side_sum), (first_sum, second_sum, third_sum) = near[0], middle[0]
    low_sum, high_sum = far[0]
    low_in, high_in, third_in = x_down(low_sum), x_up(high_sum), y_swap(third_sum)
    first_in = x_down(join(add(low(first_sum), low_in), high(first_sum)))
    second_in = x_up(join(add(low(second_sum), high_in), high(second_sum)))
    down_in = x_down(
        join(add(low(down_sum), high(first_in)), add(high(down_sum), low(third_in)))
    )
    up_in = x_up(
        join(add(low(up_sum), high(third_in)), add(high(up_sum), high(second_in)))
    )
    side_in = y_swap(
        join(add(low(side_sum), low(first_in)), add(high(side_sum), low(second_in)))
    )
    summed = add(own_sum, down_in, up_in, side_in)

    leaving = pack(low(summed), core_swap(high(summed)))
    pieces = (own, down, up, side, far_low, far_high, first, second, third)
    acts = [(call[1], call[2]) for call in (near, far, middle)]
    leaving, probs, pieces, acts = lax.optimization_barrier((leaving, probs, pieces, acts))
    probs = hold(probs)
    grad_in, grad_out = weight_grads(pieces, [a[0] for a in acts], [a[1] for a in acts])
    returned = exchange(leaving.reshape(16, 8, D), COLUMN).reshape(128, D)
    near_by = lax.optimization_barrier((tokens, cotangent, grad_in))
    near_by = hold_inputs(near_by[0], near_by[1])
    returned, near_by, grad_in = lax.optimization_barrier((returned, near_by, grad_in))
    gates, term = gate(core, returned, near_by[0], near_by[1], probs)
    grad_router = sum_over_all(term)
    output, grad_tokens = spread(core, returned, gates, probs, router)

    return (output, grad_tokens, grad_router, grad_in[None], grad_out[None])


def solution(mesh):
    fine = Mesh(mesh.devices.reshape(2, 4, 2, 8, 2), AXES)
    images = P(AXES, None, None)
    placed = (images, P(), P(EXPERT, None, DP), P(EXPERT, DP, None), images)
    return jax.shard_map(
        shards,
        mesh=fine,
        in_specs=placed,
        out_specs=(images, images, P(), placed[2], placed[3]),
        check_vma=False,
    )
```

```python
import functools

import jax
import jax.numpy as jnp
from jax import lax
from jax.experimental import pallas as pl
from jax.experimental.pallas import tpu as pltpu
from jax.sharding import Mesh, PartitionSpec as P

BF16 = jnp.bfloat16
F32 = jnp.float32
D = 1280
M = 256
SLOTS = 32
HID = 640
AXES = ("yl", "x", "yh", "z", "c")
DP = ("yl", "x")
EXPERT = ("yh", "z", "c")
PLANE = ("yl", "x", "c")
COLUMN = ("yh", "z")
VMEM = pl.BlockSpec(memory_space=pltpu.VMEM)
SMEM = pl.BlockSpec(memory_space=pltpu.SMEM)
PARAMS = pltpu.CompilerParams(vmem_limit_bytes=16 * 2**20)


def cost(flops, size):
    return pl.CostEstimate(flops=flops, bytes_accessed=size, transcendentals=0)


def mm(a, b):
    return jnp.dot(a, b, preferred_element_type=F32)


def mm_nt(a, b):
    return lax.dot_general(a, b, (((1,), (1,)), ((), ())), preferred_element_type=F32)


def mm_tn(a, b):
    return lax.dot_general(a, b, (((0,), (0,)), ((), ())), preferred_element_type=F32)


def add(*terms):
    total = terms[0].astype(F32)
    for term in terms[1:]:
        total = total + term.astype(F32)
    return total.astype(BF16)


def exchange(x, axes):
    return lax.all_to_all(x, axes, split_axis=0, concat_axis=0, tiled=True)


def x_up(a):
    return lax.ppermute(a, "x", [(i, (i + 1) % 4) for i in range(4)])


def x_down(a):
    return lax.ppermute(a, "x", [(i, (i + 3) % 4) for i in range(4)])


def y_swap(a):
    return lax.ppermute(a, "yl", [(0, 1), (1, 0)])


def core_swap(a):
    return lax.ppermute(a, "c", [(0, 1), (1, 0)])


def natural_row(r, core):
    slot = 2 * (r >> 3) + (((r >> 2) & 1) ^ core)
    return ((r >> 1) & 1) * 64 + (r & 1) * 32 + slot


def to_message(core, rows):
    r = lax.broadcasted_iota(jnp.int32, (128, 128), 0)
    n = lax.broadcasted_iota(jnp.int32, (128, 128), 1)
    pick = (n == natural_row(r, core)).astype(F32).astype(BF16)
    return mm(pick, rows).astype(BF16)


def from_message(core, message):
    n = lax.broadcasted_iota(jnp.int32, (128, 128), 0)
    r = lax.broadcasted_iota(jnp.int32, (128, 128), 1)
    pick = (n == natural_row(r, core)).astype(F32).astype(BF16)
    return mm(pick, message).astype(BF16)


def route_kernel(core, tokens, router, cotangent, message, probs, rows):
    image = pl.program_id(0)
    tok = tokens[0]
    logits = mm_nt(router[...], tok)
    disp = jnp.exp(logits - jnp.max(logits, axis=1, keepdims=True))
    disp = disp / jnp.sum(disp, axis=1, keepdims=True)
    comb = jnp.exp(logits - jnp.max(logits, axis=0, keepdims=True))
    comb = comb / jnp.sum(comb, axis=0, keepdims=True)
    probs[0, 0] = disp
    probs[0, 1] = comb
    first = pl.multiple_of(image * SLOTS, SLOTS)
    rows[pl.ds(first, SLOTS), :] = mm(disp.astype(BF16), tok).astype(BF16)
    rows[pl.ds(64 + first, SLOTS), :] = mm(comb.astype(BF16), cotangent[0]).astype(BF16)

    @pl.when(image == 1)
    def _():
        message[...] = to_message(core[0], rows[...])


def route(core, tokens, router, cotangent):
    image = pl.BlockSpec((1, M, D), lambda b: (b, 0, 0))
    probs = pl.BlockSpec((1, 2, SLOTS, M), lambda b: (b, 0, 0, 0))
    return pl.pallas_call(
        route_kernel,
        grid=(2,),
        in_specs=[SMEM, image, pl.BlockSpec((SLOTS, D), lambda b: (0, 0)), image],
        out_specs=[pl.BlockSpec((128, D), lambda b: (0, 0)), probs],
        out_shape=[
            jax.ShapeDtypeStruct((128, D), BF16),
            jax.ShapeDtypeStruct((2, 2, SLOTS, M), F32),
        ],
        scratch_shapes=[pltpu.VMEM((128, D), BF16)],
        compiler_params=pltpu.CompilerParams(vmem_limit_bytes=56 * 2**20),
        cost_estimate=cost(10**9, 3 * 10**6),
    )(core, tokens, router, cotangent)


def experts_kernel(n, order, *refs):
    held, (w_in, w_out) = refs[:n], refs[n : n + 2]
    sent, (hidden, grad_preact) = refs[n + 2 : 2 * n + 2], refs[2 * n + 2 :]
    rows = jnp.concatenate([h[:, :D] for h in held], axis=0)
    grad_rows = jnp.concatenate([h[:, D:] for h in held], axis=0)
    x = mm(rows, w_in[...])
    square = x * x
    scale = 0.7978845608028654
    t = jnp.tanh(scale * (x + 0.044715 * (square * x)))
    half = 0.5 * (1.0 + t)
    hid = (x * half).astype(BF16)
    slope = half + 0.5 * x * (1.0 - t * t) * (scale * (1.0 + 0.134145 * square))
    hidden[...] = hid
    grad = (mm_nt(grad_rows, w_out[...]) * slope).astype(BF16)
    grad_preact[...] = grad
    out = mm(hid, w_out[...]).astype(BF16)
    inner = mm_nt(grad, w_in[...]).astype(BF16)
    first = 0
    for s in sent:
        for at in range(0, s.shape[0], 32):
            block = order[first] * 32
            s[at : at + 32, :D] = out[block : block + 32]
            s[at : at + 32, D:] = inner[block : block + 32]
            first += 1


def experts(held, w_in, w_out, order=None):
    n = len(held)
    total = sum(h.shape[0] for h in held)
    order = order or tuple(range(total // 32))
    shapes = [jax.ShapeDtypeStruct(h.shape, BF16) for h in held]
    shapes += [jax.ShapeDtypeStruct((total, HID), BF16)] * 2
    results = pl.pallas_call(
        functools.partial(experts_kernel, n, order),
        in_specs=[VMEM] * (n + 2),
        out_specs=[VMEM] * (n + 2),
        out_shape=shapes,
        compiler_params=PARAMS,
        cost_estimate=cost(8 * total * D * HID, 4 * 10**6),
    )(*held, w_in, w_out)
    return results[:n], results[n], results[n + 1]


def grads_kernel(n, m, *refs):
    pieces, acts, (grad_in, grad_out) = refs[:n], refs[n : n + 2 * m], refs[n + 2 * m :]
    rows = jnp.concatenate([p[:, :D] for p in pieces], axis=0)
    grad_preact = jnp.concatenate([a[...] for a in acts[m:]], axis=0)
    grad_in[...] = mm_tn(rows, grad_preact).astype(BF16)
    hidden = jnp.concatenate([a[...] for a in acts[:m]], axis=0)
    grad_rows = jnp.concatenate([p[:, D:] for p in pieces], axis=0)
    grad_out[...] = mm_tn(hidden, grad_rows).astype(BF16)


def weight_grads(pieces, hidden, grad_preact):
    n, m = len(pieces), len(hidden)
    return pl.pallas_call(
        functools.partial(grads_kernel, n, m),
        in_specs=[VMEM] * (n + 2 * m),
        out_specs=[VMEM] * 2,
        out_shape=[
            jax.ShapeDtypeStruct((D, HID), BF16),
            jax.ShapeDtypeStruct((HID, D), BF16),
        ],
        compiler_params=PARAMS,
        cost_estimate=cost(4 * 512 * D * HID, 8 * 10**6),
    )(*pieces, *hidden, *grad_preact)


def pack_kernel(stay, go, message):
    rows = jnp.concatenate([stay[:, :D], stay[:, D:], go[:, :D], go[:, D:]], axis=0)
    r = lax.broadcasted_iota(jnp.int32, (128, 128), 0)
    n = lax.broadcasted_iota(jnp.int32, (128, 128), 1)
    pick = n == ((r >> 2) & 1) * 64 + ((r >> 1) & 1) * 32 + (r >> 3) * 2 + (r & 1)
    message[...] = mm(pick.astype(F32).astype(BF16), rows).astype(BF16)


def pack(stay, go):
    return pl.pallas_call(
        pack_kernel,
        in_specs=[VMEM] * 2,
        out_specs=VMEM,
        out_shape=jax.ShapeDtypeStruct((128, D), BF16),
        compiler_params=PARAMS,
        cost_estimate=cost(10**8, 10**6),
    )(stay, go)


def hold_kernel(probs, out):
    out[...] = probs[...]


def hold(probs):
    return pl.pallas_call(
        hold_kernel,
        in_specs=[VMEM],
        out_specs=VMEM,
        out_shape=jax.ShapeDtypeStruct(probs.shape, F32),
        compiler_params=PARAMS,
        cost_estimate=cost(10**6, 10**6),
    )(probs)


def hold_inputs_kernel(tokens, cotangent, tokens_out, cotangent_out):
    tokens_out[...] = tokens[...]
    cotangent_out[...] = cotangent[...]


def hold_inputs(tokens, cotangent):
    return pl.pallas_call(
        hold_inputs_kernel,
        in_specs=[VMEM] * 2,
        out_specs=[VMEM] * 2,
        out_shape=[jax.ShapeDtypeStruct((2, M, D), BF16)] * 2,
        compiler_params=PARAMS,
        cost_estimate=cost(10**6, 5 * 10**6),
    )(tokens, cotangent)


def gate_kernel(core, message, tokens, cotangent, probs, gates, term):
    rows = from_message(core[0], message[...])
    total = jnp.zeros((SLOTS, D), F32)
    for b in range(2):
        disp, comb = probs[b, 0], probs[b, 1]
        grad_comb = mm_nt(rows[b * 32 : b * 32 + 32], cotangent[b])
        grad_disp = mm_nt(rows[64 + b * 32 : 96 + b * 32], tokens[b])
        grad = comb * (grad_comb - jnp.sum(comb * grad_comb, axis=0, keepdims=True))
        grad += disp * (grad_disp - jnp.sum(disp * grad_disp, axis=1, keepdims=True))
        grad = grad.astype(BF16)
        gates[b] = grad
        total += mm(grad, tokens[b])
    total = total.astype(BF16)
    for e in range(16):
        term[e] = total[2 * e : 2 * e + 2]


def gate(core, message, tokens, cotangent, probs):
    return pl.pallas_call(
        gate_kernel,
        in_specs=[SMEM] + [VMEM] * 4,
        out_specs=[VMEM] * 2,
        out_shape=[
            jax.ShapeDtypeStruct((2, SLOTS, M), BF16),
            jax.ShapeDtypeStruct((16, 2, D), BF16),
        ],
        compiler_params=PARAMS,
        cost_estimate=cost(10**9, 3 * 10**6),
    )(core, message, tokens, cotangent, probs)


def spread_kernel(core, message, gates, probs, router, output, grad_tokens, rows):
    image = pl.program_id(0)

    @pl.when(image == 0)
    def _():
        rows[...] = from_message(core[0], message[...])

    first = pl.multiple_of(image * SLOTS, SLOTS)
    slots_out = rows[pl.ds(first, SLOTS), :]
    grad_slots_in = rows[pl.ds(64 + first, SLOTS), :]
    output[0] = mm_tn(probs[0, 1].astype(BF16), slots_out).astype(BF16)
    grad = mm_tn(probs[0, 0].astype(BF16), grad_slots_in) + mm_tn(gates[0], router[...])
    grad_tokens[0] = grad.astype(BF16)


def spread(core, message, gates, probs, router):
    image = pl.BlockSpec((1, M, D), lambda b: (b, 0, 0))
    return pl.pallas_call(
        spread_kernel,
        grid=(2,),
        in_specs=[
            SMEM,
            pl.BlockSpec((128, D), lambda b: (0, 0)),
            pl.BlockSpec((1, SLOTS, M), lambda b: (b, 0, 0)),
            pl.BlockSpec((1, 2, SLOTS, M), lambda b: (b, 0, 0, 0)),
            pl.BlockSpec((SLOTS, D), lambda b: (0, 0)),
        ],
        out_specs=[image, image],
        out_shape=[jax.ShapeDtypeStruct((2, M, D), BF16)] * 2,
        scratch_shapes=[pltpu.VMEM((128, D), BF16)],
        compiler_params=PARAMS,
        cost_estimate=cost(10**9, 3 * 10**6),
    )(core, message, gates, probs, router)


def low(a):
    return a[:32]


def high(a):
    return a[32:]


def join(a, b):
    return jnp.concatenate([a, b])


def fold_kernel(parts, out):
    total = parts[0].astype(F32)
    for k in range(1, 16):
        total += parts[k].astype(F32)
    total = total.astype(BF16)
    for k in range(16):
        out[k] = total


def fold(parts):
    return pl.pallas_call(
        fold_kernel,
        in_specs=[VMEM],
        out_specs=VMEM,
        out_shape=jax.ShapeDtypeStruct((16, 2, D), BF16),
        compiler_params=PARAMS,
        cost_estimate=cost(10**6, 10**6),
    )(parts)


def sum_over_all(term):
    part = exchange(fold(exchange(term, PLANE)), COLUMN)
    return exchange(fold(part), PLANE).reshape(SLOTS, D).astype(F32)


def shards(tokens, router, w_in, w_out, cotangent):
    core = lax.axis_index("c").astype(jnp.int32).reshape(1)
    w_in, w_out = w_in[0], w_out[0]
    message, probs = route(core, tokens, router, cotangent)

    arrived = exchange(message.reshape(16, 8, D), COLUMN)
    arrived = arrived.reshape(16, 2, 2, 2, D).transpose(1, 0, 3, 2, 4).reshape(2, 32, 2 * D)
    own = join(arrived[0], core_swap(arrived[1]))

    down, up, side = x_up(own), x_down(own), y_swap(own)
    first = x_up(join(low(side), low(down)))
    third = y_swap(join(high(down), high(up)))
    near = experts((own, down, up, side), w_in, w_out)
    late, near = lax.optimization_barrier((join(low(side), high(up)), near))
    second = x_down(late)
    far_low = x_up(low(first))
    far_high = x_down(high(third))
    far = experts((far_low, far_high), w_in, w_out)
    first, far = lax.optimization_barrier((first, far))
    middle = experts((first, second, third), w_in, w_out, (0, 1, 5, 3, 4, 2))

    (own_sum, down_sum, up_sum, side_sum), (first_sum, second_sum, third_sum) = near[0], middle[0]
    low_sum, high_sum = far[0]
    low_in, high_in, third_in = x_down(low_sum), x_up(high_sum), y_swap(third_sum)
    first_in = x_down(join(add(low(first_sum), low_in), high(first_sum)))
    second_in = x_up(join(add(low(second_sum), high_in), high(second_sum)))
    down_in = x_down(
        join(add(low(down_sum), high(first_in)), add(high(down_sum), low(third_in)))
    )
    up_in = x_up(
        join(add(low(up_sum), high(third_in)), add(high(up_sum), high(second_in)))
    )
    side_in = y_swap(
        join(add(low(side_sum), low(first_in)), add(high(side_sum), low(second_in)))
    )
    summed = add(own_sum, down_in, up_in, side_in)

    leaving = pack(low(summed), core_swap(high(summed)))
    pieces = (own, down, up, side, far_low, far_high, first, second, third)
    acts = [(call[1], call[2]) for call in (near, far, middle)]
    leaving, probs, pieces, acts = lax.optimization_barrier((leaving, probs, pieces, acts))
    probs = hold(probs)
    grad_in, grad_out = weight_grads(pieces, [a[0] for a in acts], [a[1] for a in acts])
    returned = exchange(leaving.reshape(16, 8, D), COLUMN).reshape(128, D)
    near_by = lax.optimization_barrier((tokens, cotangent, grad_in))
    near_by = hold_inputs(near_by[0], near_by[1])
    returned, near_by, grad_in = lax.optimization_barrier((returned, near_by, grad_in))
    gates, term = gate(core, returned, near_by[0], near_by[1], probs)
    grad_router = sum_over_all(term)
    output, grad_tokens = spread(core, returned, gates, probs, router)

    return (output, grad_tokens, grad_router, grad_in[None], grad_out[None])


def solution(mesh):
    fine = Mesh(mesh.devices.reshape(2, 4, 2, 8, 2), AXES)
    images = P(AXES, None, None)
    placed = (images, P(), P(EXPERT, None, DP), P(EXPERT, DP, None), images)
    return jax.shard_map(
        shards,
        mesh=fine,
        in_specs=placed,
        out_specs=(images, images, P(), placed[2], placed[3]),
        check_vma=False,
    )
```

```python
import functools

import jax
import jax.numpy as jnp
from jax import lax
from jax.experimental import pallas as pl
from jax.experimental.pallas import tpu as pltpu
from jax.sharding import Mesh, PartitionSpec as P

BF16 = jnp.bfloat16
F32 = jnp.float32
D = 1280
M = 256
SLOTS = 32
HID = 640
AXES = ("yl", "x", "yh", "z", "c")
DP = ("yl", "x")
EXPERT = ("yh", "z", "c")
PLANE = ("yl", "x", "c")
COLUMN = ("yh", "z")
VMEM = pl.BlockSpec(memory_space=pltpu.VMEM)
SMEM = pl.BlockSpec(memory_space=pltpu.SMEM)
PARAMS = pltpu.CompilerParams(vmem_limit_bytes=16 * 2**20)


def cost(flops, size):
    return pl.CostEstimate(flops=flops, bytes_accessed=size, transcendentals=0)


def mm(a, b):
    return jnp.dot(a, b, preferred_element_type=F32)


def mm_nt(a, b):
    return lax.dot_general(a, b, (((1,), (1,)), ((), ())), preferred_element_type=F32)


def mm_tn(a, b):
    return lax.dot_general(a, b, (((0,), (0,)), ((), ())), preferred_element_type=F32)


def add(*terms):
    total = terms[0].astype(F32)
    for term in terms[1:]:
        total = total + term.astype(F32)
    return total.astype(BF16)


def exchange(x, axes):
    return lax.all_to_all(x, axes, split_axis=0, concat_axis=0, tiled=True)


def x_up(a):
    return lax.ppermute(a, "x", [(i, (i + 1) % 4) for i in range(4)])


def x_down(a):
    return lax.ppermute(a, "x", [(i, (i + 3) % 4) for i in range(4)])


def y_swap(a):
    return lax.ppermute(a, "yl", [(0, 1), (1, 0)])


def core_swap(a):
    return lax.ppermute(a, "c", [(0, 1), (1, 0)])


def natural_row(r, core):
    slot = 2 * (r >> 3) + (((r >> 2) & 1) ^ core)
    return ((r >> 1) & 1) * 64 + (r & 1) * 32 + slot


def to_message(core, rows):
    r = lax.broadcasted_iota(jnp.int32, (128, 128), 0)
    n = lax.broadcasted_iota(jnp.int32, (128, 128), 1)
    pick = (n == natural_row(r, core)).astype(F32).astype(BF16)
    return mm(pick, rows).astype(BF16)


def from_message(core, message):
    n = lax.broadcasted_iota(jnp.int32, (128, 128), 0)
    r = lax.broadcasted_iota(jnp.int32, (128, 128), 1)
    pick = (n == natural_row(r, core)).astype(F32).astype(BF16)
    return mm(pick, message).astype(BF16)


def route_kernel(core, tokens, router, cotangent, message, probs, rows):
    image = pl.program_id(0)
    tok = tokens[0]
    logits = mm_nt(router[...], tok)
    disp = jnp.exp(logits - jnp.max(logits, axis=1, keepdims=True))
    disp = disp / jnp.sum(disp, axis=1, keepdims=True)
    comb = jnp.exp(logits - jnp.max(logits, axis=0, keepdims=True))
    comb = comb / jnp.sum(comb, axis=0, keepdims=True)
    probs[0, 0] = disp
    probs[0, 1] = comb
    first = pl.multiple_of(image * SLOTS, SLOTS)
    rows[pl.ds(first, SLOTS), :] = mm(disp.astype(BF16), tok).astype(BF16)
    rows[pl.ds(64 + first, SLOTS), :] = mm(comb.astype(BF16), cotangent[0]).astype(BF16)

    @pl.when(image == 1)
    def _():
        message[...] = to_message(core[0], rows[...])


def route(core, tokens, router, cotangent):
    image = pl.BlockSpec((1, M, D), lambda b: (b, 0, 0))
    probs = pl.BlockSpec((1, 2, SLOTS, M), lambda b: (b, 0, 0, 0))
    return pl.pallas_call(
        route_kernel,
        grid=(2,),
        in_specs=[SMEM, image, pl.BlockSpec((SLOTS, D), lambda b: (0, 0)), image],
        out_specs=[pl.BlockSpec((128, D), lambda b: (0, 0)), probs],
        out_shape=[
            jax.ShapeDtypeStruct((128, D), BF16),
            jax.ShapeDtypeStruct((2, 2, SLOTS, M), F32),
        ],
        scratch_shapes=[pltpu.VMEM((128, D), BF16)],
        compiler_params=pltpu.CompilerParams(vmem_limit_bytes=56 * 2**20),
        cost_estimate=cost(10**9, 3 * 10**6),
    )(core, tokens, router, cotangent)


def experts_kernel(n, order, *refs):
    held, (w_in, w_out) = refs[:n], refs[n : n + 2]
    sent, (hidden, grad_preact) = refs[n + 2 : 2 * n + 2], refs[2 * n + 2 :]
    rows = jnp.concatenate([h[:, :D] for h in held], axis=0)
    grad_rows = jnp.concatenate([h[:, D:] for h in held], axis=0)
    x = mm(rows, w_in[...])
    square = x * x
    scale = 0.7978845608028654
    t = jnp.tanh(scale * (x + 0.044715 * (square * x)))
    half = 0.5 * (1.0 + t)
    hid = (x * half).astype(BF16)
    slope = half + 0.5 * x * (1.0 - t * t) * (scale * (1.0 + 0.134145 * square))
    hidden[...] = hid
    grad = (mm_nt(grad_rows, w_out[...]) * slope).astype(BF16)
    grad_preact[...] = grad
    out = mm(hid, w_out[...]).astype(BF16)
    inner = mm_nt(grad, w_in[...]).astype(BF16)
    first = 0
    for s in sent:
        for at in range(0, s.shape[0], 32):
            block = order[first] * 32
            s[at : at + 32, :D] = out[block : block + 32]
            s[at : at + 32, D:] = inner[block : block + 32]
            first += 1


def experts(held, w_in, w_out, order=None):
    n = len(held)
    total = sum(h.shape[0] for h in held)
    order = order or tuple(range(total // 32))
    shapes = [jax.ShapeDtypeStruct(h.shape, BF16) for h in held]
    shapes += [jax.ShapeDtypeStruct((total, HID), BF16)] * 2
    results = pl.pallas_call(
        functools.partial(experts_kernel, n, order),
        in_specs=[VMEM] * (n + 2),
        out_specs=[VMEM] * (n + 2),
        out_shape=shapes,
        compiler_params=PARAMS,
        cost_estimate=cost(8 * total * D * HID, 4 * 10**6),
    )(*held, w_in, w_out)
    return results[:n], results[n], results[n + 1]


def grads_kernel(n, m, *refs):
    pieces, acts, (grad_in, grad_out) = refs[:n], refs[n : n + 2 * m], refs[n + 2 * m :]
    rows = jnp.concatenate([p[:, :D] for p in pieces], axis=0)
    grad_preact = jnp.concatenate([a[...] for a in acts[m:]], axis=0)
    grad_in[...] = mm_tn(rows, grad_preact).astype(BF16)
    hidden = jnp.concatenate([a[...] for a in acts[:m]], axis=0)
    grad_rows = jnp.concatenate([p[:, D:] for p in pieces], axis=0)
    grad_out[...] = mm_tn(hidden, grad_rows).astype(BF16)


def weight_grads(pieces, hidden, grad_preact):
    n, m = len(pieces), len(hidden)
    return pl.pallas_call(
        functools.partial(grads_kernel, n, m),
        in_specs=[VMEM] * (n + 2 * m),
        out_specs=[VMEM] * 2,
        out_shape=[
            jax.ShapeDtypeStruct((D, HID), BF16),
            jax.ShapeDtypeStruct((HID, D), BF16),
        ],
        compiler_params=PARAMS,
        cost_estimate=cost(4 * 512 * D * HID, 8 * 10**6),
    )(*pieces, *hidden, *grad_preact)


def pack_kernel(own, down, up, side, go, message):
    stay = add(own[:32], down[:32], up[:32], side[:32])
    rows = jnp.concatenate([stay[:, :D], stay[:, D:], go[:, :D], go[:, D:]], axis=0)
    r = lax.broadcasted_iota(jnp.int32, (128, 128), 0)
    n = lax.broadcasted_iota(jnp.int32, (128, 128), 1)
    pick = n == ((r >> 2) & 1) * 64 + ((r >> 1) & 1) * 32 + (r >> 3) * 2 + (r & 1)
    message[...] = mm(pick.astype(F32).astype(BF16), rows).astype(BF16)


def pack(own, down, up, side, go):
    return pl.pallas_call(
        pack_kernel,
        in_specs=[VMEM] * 5,
        out_specs=VMEM,
        out_shape=jax.ShapeDtypeStruct((128, D), BF16),
        compiler_params=PARAMS,
        cost_estimate=cost(10**8, 10**6),
    )(own, down, up, side, go)


def hold_kernel(probs, out):
    out[...] = probs[...]


def hold(probs):
    return pl.pallas_call(
        hold_kernel,
        in_specs=[VMEM],
        out_specs=VMEM,
        out_shape=jax.ShapeDtypeStruct(probs.shape, F32),
        compiler_params=PARAMS,
        cost_estimate=cost(10**6, 10**6),
    )(probs)


def hold_inputs_kernel(tokens, cotangent, tokens_out, cotangent_out):
    tokens_out[...] = tokens[...]
    cotangent_out[...] = cotangent[...]


def hold_inputs(tokens, cotangent):
    return pl.pallas_call(
        hold_inputs_kernel,
        in_specs=[VMEM] * 2,
        out_specs=[VMEM] * 2,
        out_shape=[jax.ShapeDtypeStruct((2, M, D), BF16)] * 2,
        compiler_params=PARAMS,
        cost_estimate=cost(10**6, 5 * 10**6),
    )(tokens, cotangent)


def gate_kernel(core, message, tokens, cotangent, probs, gates, term):
    rows = from_message(core[0], message[...])
    total = jnp.zeros((SLOTS, D), F32)
    for b in range(2):
        disp, comb = probs[b, 0], probs[b, 1]
        grad_comb = mm_nt(rows[b * 32 : b * 32 + 32], cotangent[b])
        grad_disp = mm_nt(rows[64 + b * 32 : 96 + b * 32], tokens[b])
        grad = comb * (grad_comb - jnp.sum(comb * grad_comb, axis=0, keepdims=True))
        grad += disp * (grad_disp - jnp.sum(disp * grad_disp, axis=1, keepdims=True))
        grad = grad.astype(BF16)
        gates[b] = grad
        total += mm(grad, tokens[b])
    total = total.astype(BF16)
    for e in range(16):
        term[e] = total[2 * e : 2 * e + 2]


def gate(core, message, tokens, cotangent, probs):
    return pl.pallas_call(
        gate_kernel,
        in_specs=[SMEM] + [VMEM] * 4,
        out_specs=[VMEM] * 2,
        out_shape=[
            jax.ShapeDtypeStruct((2, SLOTS, M), BF16),
            jax.ShapeDtypeStruct((16, 2, D), BF16),
        ],
        compiler_params=PARAMS,
        cost_estimate=cost(10**9, 3 * 10**6),
    )(core, message, tokens, cotangent, probs)


def spread_kernel(core, message, gates, probs, router, output, grad_tokens, rows):
    image = pl.program_id(0)

    @pl.when(image == 0)
    def _():
        rows[...] = from_message(core[0], message[...])

    first = pl.multiple_of(image * SLOTS, SLOTS)
    slots_out = rows[pl.ds(first, SLOTS), :]
    grad_slots_in = rows[pl.ds(64 + first, SLOTS), :]
    output[0] = mm_tn(probs[0, 1].astype(BF16), slots_out).astype(BF16)
    grad = mm_tn(probs[0, 0].astype(BF16), grad_slots_in) + mm_tn(gates[0], router[...])
    grad_tokens[0] = grad.astype(BF16)


def spread(core, message, gates, probs, router):
    image = pl.BlockSpec((1, M, D), lambda b: (b, 0, 0))
    return pl.pallas_call(
        spread_kernel,
        grid=(2,),
        in_specs=[
            SMEM,
            pl.BlockSpec((128, D), lambda b: (0, 0)),
            pl.BlockSpec((1, SLOTS, M), lambda b: (b, 0, 0)),
            pl.BlockSpec((1, 2, SLOTS, M), lambda b: (b, 0, 0, 0)),
            pl.BlockSpec((SLOTS, D), lambda b: (0, 0)),
        ],
        out_specs=[image, image],
        out_shape=[jax.ShapeDtypeStruct((2, M, D), BF16)] * 2,
        scratch_shapes=[pltpu.VMEM((128, D), BF16)],
        compiler_params=PARAMS,
        cost_estimate=cost(10**9, 3 * 10**6),
    )(core, message, gates, probs, router)


def low(a):
    return a[:32]


def high(a):
    return a[32:]


def join(a, b):
    return jnp.concatenate([a, b])


def sum_over_all(term):
    part = exchange(term, PLANE)
    part = jnp.sum(part.astype(F32), axis=0).astype(BF16)
    part = exchange(jnp.broadcast_to(part[None], (16, 2, D)), COLUMN)
    part = jnp.sum(part.astype(F32), axis=0).astype(BF16)
    part = exchange(jnp.broadcast_to(part[None], (16, 2, D)), PLANE)
    return part.reshape(SLOTS, D).astype(F32)


def shards(tokens, router, w_in, w_out, cotangent):
    core = lax.axis_index("c").astype(jnp.int32).reshape(1)
    w_in, w_out = w_in[0], w_out[0]
    message, probs = route(core, tokens, router, cotangent)

    arrived = exchange(message.reshape(16, 8, D), COLUMN)
    arrived = arrived.reshape(16, 2, 2, 2, D).transpose(1, 0, 3, 2, 4).reshape(2, 32, 2 * D)
    own = join(arrived[0], core_swap(arrived[1]))

    down, up, side = x_up(own), x_down(own), y_swap(own)
    first = x_up(join(low(side), low(down)))
    third = y_swap(join(high(down), high(up)))
    near = experts((own, down, up, side), w_in, w_out)
    late, near = lax.optimization_barrier((join(low(side), high(up)), near))
    second = x_down(late)
    far_low = x_up(low(first))
    far_high = x_down(high(third))
    far = experts((far_low, far_high), w_in, w_out)
    first, far = lax.optimization_barrier((first, far))
    middle = experts((first, second, third), w_in, w_out, (0, 1, 5, 3, 4, 2))

    (own_sum, down_sum, up_sum, side_sum), (first_sum, second_sum, third_sum) = near[0], middle[0]
    low_sum, high_sum = far[0]
    low_in, high_in, third_in = x_down(low_sum), x_up(high_sum), y_swap(third_sum)
    first_in = x_down(join(add(low(first_sum), low_in), high(first_sum)))
    second_in = x_up(join(add(low(second_sum), high_in), high(second_sum)))
    down_in = x_down(
        join(add(low(down_sum), high(first_in)), add(high(down_sum), low(third_in)))
    )
    up_in = x_up(
        join(add(low(up_sum), high(third_in)), add(high(up_sum), high(second_in)))
    )
    side_in = y_swap(
        join(add(low(side_sum), low(first_in)), add(high(side_sum), low(second_in)))
    )
    go = core_swap(add(high(own_sum), high(down_in), high(up_in), high(side_in)))
    leaving = pack(own_sum, down_in, up_in, side_in, go)
    pieces = (own, down, up, side, far_low, far_high, first, second, third)
    acts = [(call[1], call[2]) for call in (near, far, middle)]
    leaving, probs, pieces, acts = lax.optimization_barrier((leaving, probs, pieces, acts))
    probs = hold(probs)
    grad_in, grad_out = weight_grads(pieces, [a[0] for a in acts], [a[1] for a in acts])
    returned = exchange(leaving.reshape(16, 8, D), COLUMN).reshape(128, D)
    near_by = lax.optimization_barrier((tokens, cotangent, grad_in))
    near_by = hold_inputs(near_by[0], near_by[1])
    returned, near_by, grad_in = lax.optimization_barrier((returned, near_by, grad_in))
    gates, term = gate(core, returned, near_by[0], near_by[1], probs)
    grad_router = sum_over_all(term)
    output, grad_tokens = spread(core, returned, gates, probs, router)

    return (output, grad_tokens, grad_router, grad_in[None], grad_out[None])


def solution(mesh):
    fine = Mesh(mesh.devices.reshape(2, 4, 2, 8, 2), AXES)
    images = P(AXES, None, None)
    placed = (images, P(), P(EXPERT, None, DP), P(EXPERT, DP, None), images)
    return jax.shard_map(
        shards,
        mesh=fine,
        in_specs=placed,
        out_specs=(images, images, P(), placed[2], placed[3]),
        check_vma=False,
    )
```
